32 devices in a mesh: groups: 2 (over y), ctx: 4 (over z), head: 2 (over x), rep: 2 (over core).
Axes of the slice: x: 2, y: 2, z: 4, core: 2. Of those that a mesh axis runs over, the one named last changes fastest.
Arguments:
- queries: bfloat16 [4, 512, 1024], P(('groups', 'rep'), 'ctx', 'head'), parts along dimension 0, may hold values from -6 to 6
- per_head_keys: bfloat16 [4, 512, 1024], P(('groups', 'rep'), 'ctx', 'head'), parts along dimension 0, may hold values from -6 to 6
- value_rows: bfloat16 [4, 512, 1024], P(('groups', 'rep'), 'ctx', 'head'), parts along dimension 0, may hold values from -6 to 6
- gate_logits: bfloat16 [4, 512, 1024], P(('groups', 'rep'), 'ctx', 'head'), parts along dimension 0, may hold values from -16 to 4
- gate_bias: float32 [1024], P('head'), may hold values from -1 to 13
- value_weight: float32 [1024], P('head'), may hold values from -0.1875 to 0.1875
- targets: float32 [4, 512], P(('groups', 'rep'), 'ctx'), parts along dimension 0, may hold values from -6 to 6
- mask_ids: int32 [4, 4], P(('groups', 'rep'), 'ctx'), parts along dimension 0, may hold values from 0 to 3
- segment_starts: int32 [4, 512], P(('groups', 'rep'), 'ctx'), parts along dimension 0, may hold values 0 or 1
Outputs:
- value_pred: float32 [4, 512], P(('groups', 'rep'), 'ctx'), parts along dimension 0
- query_gradient_rows: bfloat16 [4, 512, 1024], P(('groups', 'rep'), 'ctx', 'head'), parts along dimension 0
- grad_keys: bfloat16 [4, 512, 1024], P(('groups', 'rep'), 'ctx', 'head'), parts along dimension 0
- grad_values: bfloat16 [4, 512, 1024], P(('groups', 'rep'), 'ctx', 'head'), parts along dimension 0
- grad_gate_logits: bfloat16 [4, 512, 1024], P(('groups', 'rep'), 'ctx', 'head'), parts along dimension 0
- grad_gate_bias: float32 [2048], P(('groups', 'head')), parts along dimension 0
- grad_value_weight: float32 [2048], P(('groups', 'head')), parts along dimension 0
The draws below stay inside these ranges and needn't reach their ends.
There are 2 independent parts, one for each index of `groups`. The reference program is written for one: setup_inputs(seed, part) draws one part's arguments, and reference() takes and returns one part's arrays. A program takes and returns all parts, laid end to end along the dimension named above; an argument that names none is the same for every part. Nothing has to cross between parts.
Inputs may be any that keep to these rules, and one draw needn't show every extreme that they name: `mask_ids`: the window kind of each block of 128 positions. `segment_starts`: flags of segment starts.
All inputs are finite; a program needn't handle non-finite values. No bound on the sum of `segment_starts` on one device may be relied on, other than what follows from the above.
Results may differ from the reference program's by a relative error of at most 0.013.
Values sent between devices are 32-bit elements; how exact they have to be, the bound alone decides.
A program may use at most 64 MiB of HBM per device.

```python
import jax
import jax.numpy as jnp
from jax import lax

DK = 128
DV = 128
BLOCK = 128
TOK_DEV = 128
HEADS = 8
SEQUENCE_LENGTH = 512
SEQUENCE_GROUP = 2


def draw_gate_logits(key, part):
    first, latter_half, third = jax.random.split(key, 3)
    shape = (SEQUENCE_GROUP, SEQUENCE_LENGTH, HEADS * DK)
    start_offset = jnp.clip(jax.random.normal(first, shape, jnp.float32), -4.0, 4.0)
    position_span = jax.random.bernoulli(latter_half, 1.0 / 1024.0, (SEQUENCE_GROUP, SEQUENCE_LENGTH, 1))
    level_number = jax.random.uniform(third, (SEQUENCE_GROUP, SEQUENCE_LENGTH, 1), jnp.float32, -16.0, -12.0)
    return jnp.where(position_span, level_number, start_offset).astype(jnp.bfloat16)


def draw_gate_bias(key, part):
    first = jax.random.fold_in(key, 0)
    return jax.random.uniform(first, (HEADS * DK,), jnp.float32, -1.0, 13.0)


def with_ends(values, own_key, low, top_value):
    index_at = [jax.random.randint(jax.random.fold_in(own_key, axis), (), 0, length) for axis, length in enumerate(values.shape)]
    longest = values.shape.index(max(values.shape))
    neighbour = index_at[:longest] + [(index_at[longest] + 1) % values.shape[longest]] + index_at[longest + 1:]
    return values.at[tuple(index_at)].set(low).at[tuple(neighbour)].set(top_value)


def block_levels(key, dims, cuts, least, largest):
    gain, own = 1.0, jax.random.fold_in(key, 6)
    for axis_at, blocks in cuts:
        steps = jnp.exp(jax.random.uniform(jax.random.fold_in(own, axis_at), (blocks,), jnp.float32, least / len(cuts), largest / len(cuts)))
        gain = gain * jnp.repeat(steps, dims[axis_at] // blocks).reshape([-1 if axis == axis_at else 1 for axis in range(len(dims))])
    return gain


def scatter_about(stream_key, extent, spread, most, cuts=(), kind=jnp.bfloat16):
    drawn = jax.random.normal(stream_key, extent, jnp.float32) * spread
    if len(cuts) > 0:
        drawn = block_levels(stream_key, extent, cuts, -0.22, 0.18) * drawn
    return jnp.clip(drawn, min=-most, max=most).astype(kind)


def setup_inputs(seed: int = 0, part: int = 0) -> dict:
    key_list = jax.random.split(jax.random.key(seed), 10)
    own_keys = jax.random.split(jax.random.fold_in(key_list[9], part), 10)
    return {
        "queries": scatter_about(own_keys[0], (SEQUENCE_GROUP, SEQUENCE_LENGTH, HEADS * DK), 1.0, 6.0, ((0, 2), (1, 4), (2, 2))),
        "per_head_keys": scatter_about(own_keys[1], (SEQUENCE_GROUP, SEQUENCE_LENGTH, HEADS * DK), 1.0, 6.0, ((0, 2), (1, 4), (2, 2))),
        "value_rows": scatter_about(own_keys[2], (SEQUENCE_GROUP, SEQUENCE_LENGTH, HEADS * DV), 1.0, 6.0, ((0, 2), (1, 4), (2, 2))),
        "gate_logits": draw_gate_logits(jax.random.fold_in(jax.random.fold_in(key_list[9], part), 71), part),
        "gate_bias": draw_gate_bias(jax.random.fold_in(key_list[9], 71), part),
        "value_weight": scatter_about(key_list[5], (HEADS * DV,), (HEADS * DV) ** -0.5, 0.1875, ((0, 2),), jnp.float32),
        "targets": scatter_about(own_keys[6], (SEQUENCE_GROUP, SEQUENCE_LENGTH), 1.0, 6.0, ((0, 2), (1, 4)), jnp.float32),
        "mask_ids": with_ends(jax.random.randint(own_keys[7], (SEQUENCE_GROUP, SEQUENCE_LENGTH // BLOCK), 0, 4), jax.random.fold_in(own_keys[7], 1), 0, 3).astype(jnp.int32),
        "segment_starts": with_ends((jax.random.randint(own_keys[8], (SEQUENCE_GROUP, SEQUENCE_LENGTH), 0, 4 * TOK_DEV) < 1).astype(jnp.int32), jax.random.fold_in(own_keys[8], 1), 0, 1),
    }


epsilon = 1.0
gate_scale = 16.0
highest = lax.Precision.HIGHEST

def block_pass(query_in, key_in, value_in, decay, start_flags, kind_ids):
    blocks = kind_ids.shape[0]
    block_len = query_in.shape[0] // blocks
    head_count = query_in.shape[1]
    channels = query_in.shape[2]
    value_width = value_in.shape[2]
    query_f = query_in.astype(jnp.float32).reshape(blocks, block_len, head_count, channels)
    key_f = key_in.astype(jnp.float32).reshape(blocks, block_len, head_count, channels)
    value_f = value_in.astype(jnp.float32).reshape(blocks, block_len, head_count, value_width)
    log_cum = jnp.cumsum(decay.reshape(blocks, block_len, head_count, channels), axis=1)
    log_last = log_cum[:, -1]
    segment = jnp.cumsum(start_flags.reshape(blocks, block_len), axis=1, dtype=jnp.int32)
    alive_mask = (segment == 0).astype(jnp.float32)
    offsets = jnp.arange(block_len, dtype=jnp.int32)
    distance = offsets[:, None] - offsets[None, :]
    window = block_len // jnp.left_shift(jnp.ones_like(kind_ids), kind_ids)
    live_pairs = (segment[:, :, None] == segment[:, None, :]) & (distance[None] >= 0) & (distance[None] < window[:, None, None])
    query_dec = query_f * jnp.exp(log_cum) * channels ** (-0.5)
    key_dec = key_f * jnp.exp(-log_cum)
    scores = jnp.einsum('bihc,bjhc->bhij', query_dec, key_dec, precision=highest)
    block_probs = jnp.where(live_pairs[:, None], scores, 0.0).astype(jnp.bfloat16)
    inner_part = jnp.einsum('bhij,bjhd->bihd', block_probs.astype(jnp.float32), value_f, precision=highest)
    tail_mask = (segment == segment[:, -1:]).astype(jnp.float32)
    key_tail = key_f * jnp.exp(log_last[:, None] - log_cum) * tail_mask[:, :, None, None]
    block_state = jnp.einsum('bjhc,bjhd->bhcd', key_tail, value_f, precision=highest)
    block_decay = jnp.exp(log_last) * alive_mask[:, -1][:, None, None]

    def advance(carried_in, block_items):
        state_now, factor = carried_in
        new_state = state_now * block_items[1][..., None] + block_items[0]
        return ((new_state, factor * block_items[1]), (state_now, factor))
    initial = (jnp.zeros((head_count, channels, value_width), jnp.float32), jnp.ones((head_count, channels), jnp.float32))
    finals, befores = lax.scan(advance, initial, (block_state, block_decay))
    query_live = query_dec * alive_mask[:, :, None, None]
    outer_part = jnp.einsum('bihc,bhcd->bihd', query_live, befores[0], precision=highest)
    carried = query_live * befores[1][:, None]
    attended = (inner_part + outer_part).reshape(blocks * block_len, head_count, value_width)
    return (attended, finals[0], finals[1], carried.reshape(blocks * block_len, head_count, channels))

def head_forward(query_in, key_in, value_in, logit_in, bias_in, weight_in, segment_starts, mask_ids):

    def one_sequence(query_seq, key_seq, value_seq, logit_seq, start_seq, kind_seq):
        decay = jax.nn.log_sigmoid(logit_seq.astype(jnp.float32) + bias_in) / gate_scale
        attended = block_pass(query_seq[:, None], key_seq[:, None], value_seq[:, None], decay[:, None], start_seq, kind_seq)[0][:, 0]
        normed = attended * lax.rsqrt(lax.optimization_barrier(jnp.mean(attended * attended, axis=-1, keepdims=True)) + epsilon)
        return jnp.dot(normed, weight_in, precision=highest)
    return jax.vmap(one_sequence)(query_in, key_in, value_in, logit_in, segment_starts, mask_ids)

def reference(queries, per_head_keys, value_rows, gate_logits, gate_bias, value_weight, targets, mask_ids, segment_starts):
    sequence_count, length, feature_count = queries.shape

    def split_heads(array):
        return array.reshape(sequence_count, length, HEADS, -1).transpose(2, 0, 1, 3)

    def merge_heads(array):
        return array.transpose(1, 2, 0, 3).reshape(sequence_count, length, -1)
    per_head = (split_heads(queries), split_heads(per_head_keys), split_heads(value_rows), split_heads(gate_logits), gate_bias.reshape(HEADS, DK), value_weight.reshape(HEADS, DV))

    def forward_only(items):
        return head_forward(*items, segment_starts, mask_ids)
    value_pred = lax.optimization_barrier(jnp.sum(lax.map(forward_only, per_head), axis=0))
    residual = value_pred - targets

    def backward_head(items):

        def head_value(*inputs):
            return head_forward(*inputs, segment_starts, mask_ids)
        unused, pull = jax.vjp(head_value, *items)
        return pull(residual)
    grads = lax.map(backward_head, per_head)
    token_total = sequence_count * length
    return (value_pred, merge_heads(grads[0]), merge_heads(grads[1]), merge_heads(grads[2]), merge_heads(grads[3]), grads[4].reshape(-1) / token_total, grads[5].reshape(-1) / token_total)
```

```python
import functools

import jax
import jax.numpy as jnp
from jax import lax
from jax.experimental import pallas as pl
from jax.experimental.pallas import tpu as pltpu
from jax.sharding import PartitionSpec as P

DK = 128
DV = 128
EPSILON = 1.0
GATE_SCALE = 16.0
MESH = pl.DeviceIdType.MESH
f32 = jnp.float32
bf16 = jnp.bfloat16


def dot(a, b, da, db):
    return lax.dot_general(a, b, (((da,), (db,)), ((), ())), preferred_element_type=f32)


def split_dot(ones, x):
    hi = x.astype(bf16)
    lo = (x - hi.astype(f32)).astype(bf16)
    return dot(ones, hi, 1, 0) + dot(ones, lo, 1, 0)


def kernel(
    n_ctx, n_head, n_rep, heads,
    q_ref, k_ref, v_ref, g_ref, bias_ref, weight_ref, target_ref, kind_ref, start_ref,
    value_out, dq_out, dk_out, dv_out, dg_out, dbias_out, dweight_out,
    qd, kd, kt, vt, probs, e_up, e_down, slope, att, s_loc, s_in, g_dir, g_in,
    ptg, dqd, dkd, last, vals, red,
    s_send, s_recv, gs_send, gs_recv, v_send, v_recv, r_send, r_recv,
):
    T = q_ref.shape[1]
    ctx = lax.axis_index("ctx")
    head = lax.axis_index("head")
    rep = lax.axis_index("rep")
    n_red = n_ctx * n_rep
    me = ctx * n_rep + rep

    barrier = pltpu.get_barrier_semaphore()
    for o in range(1, n_red):
        to = lax.rem(me + o, n_red)
        pl.semaphore_signal(
            barrier, inc=1, device_id={"ctx": to // n_rep, "rep": lax.rem(to, n_rep)},
            device_id_type=MESH,
        )
    for o in range(1, n_head):
        pl.semaphore_signal(
            barrier, inc=1, device_id={"head": lax.rem(head + o, n_head)}, device_id_type=MESH
        )

    rows = lax.broadcasted_iota(jnp.int32, (T, T), 0)
    cols = lax.broadcasted_iota(jnp.int32, (T, T), 1)
    lower = (rows >= cols)
    lower_b = jnp.where(lower, 1.0, 0.0).astype(bf16)
    flags = start_ref[...].astype(f32)
    seg_col = jnp.sum(jnp.where(lower, flags, 0.0), axis=1, keepdims=True)
    seg_last = jnp.sum(flags, axis=1, keepdims=True)
    alive = jnp.where(seg_col == 0.0, 1.0, 0.0)
    tail = jnp.where(seg_col == seg_last, 1.0, 0.0)
    alive_last = jnp.where(seg_last == 0.0, 1.0, 0.0)

    def cut(h):
        return slice(h * DK, (h + 1) * DK)

    def state_copy(h):
        return pltpu.make_async_remote_copy(
            src_ref=s_loc.at[h], dst_ref=s_in.at[h], send_sem=s_send.at[h], recv_sem=s_recv.at[h],
            device_id={"ctx": lax.rem(ctx + 1, n_ctx)}, device_id_type=MESH,
        )

    def grad_copy(h):
        return pltpu.make_async_remote_copy(
            src_ref=g_dir.at[h], dst_ref=g_in.at[h], send_sem=gs_send.at[h], recv_sem=gs_recv.at[h],
            device_id={"ctx": lax.rem(ctx + n_ctx - 1, n_ctx)}, device_id_type=MESH,
        )

    for h in range(heads):
        x = g_ref[0, :, cut(h)].astype(f32) + bias_ref[:, cut(h)]
        e = jnp.exp(-jnp.abs(x))
        decay = (jnp.minimum(x, 0.0) - jnp.log(1.0 + e)) * (1.0 / GATE_SCALE)
        slope[h] = jnp.where(x >= 0.0, e, 1.0) / (1.0 + e) * (1.0 / GATE_SCALE)
        cum = split_dot(lower_b, decay)
        up = jnp.exp(cum)
        down = jnp.exp(-cum)
        e_up[h] = up * DK ** (-0.5)
        e_down[h] = down
        up_last = up[T - 1 : T, :]
        last[h : h + 1, :] = up_last
        k_dec = k_ref[0, :, cut(h)].astype(f32) * down
        kd[h] = k_dec.astype(bf16)
        tail_k = (k_dec * up_last * tail).astype(bf16)
        kt[h] = tail_k
        s_loc[h] = dot(v_ref[0, :, cut(h)], tail_k, 0, 0)

    pl.semaphore_wait(barrier, n_red + n_head - 2)

    @pl.when(ctx == 0)
    def _():
        if n_ctx > 1:
            for h in range(heads):
                state_copy(h).start()
        s_in[...] = jnp.zeros_like(s_in)

    eye = rows == cols
    start_col = jnp.sum(jnp.where(eye, flags, 0.0), axis=1, keepdims=True)
    seg_row = jnp.sum(jnp.where(rows <= cols, start_col, 0.0), axis=0, keepdims=True)
    kind = kind_ref[...]
    window = jnp.where(kind == 0, T, jnp.where(kind == 1, T // 2, jnp.where(kind == 2, T // 4, T // 8)))
    live = lower & (seg_col == seg_row) & (rows - cols < window)
    for h in range(heads):
        q_dec = (q_ref[0, :, cut(h)].astype(f32) * e_up[h]).astype(bf16)
        qd[h] = q_dec
        p = jnp.where(live, dot(q_dec, kd[h], 1, 1), 0.0).astype(bf16)
        probs[h] = p
        att[h] = dot(p, v_ref[0, :, cut(h)], 1, 0)
        vt[h] = (v_ref[0, :, cut(h)].astype(f32) * tail).astype(bf16)

    partial = jnp.zeros((T, 1), f32)
    for h in range(heads):
        if n_ctx > 1:
            @pl.when(ctx > 0)
            def _():
                state_copy(h).wait_recv()

            @pl.when((ctx > 0) & (ctx < n_ctx - 1))
            def _():
                s_loc[h] = s_in[h] * (last[h : h + 1, :] * alive_last) + s_loc[h]
                state_copy(h).start()

        a = att[h] + dot(qd[h], s_in[h].astype(bf16), 1, 1) * alive
        att[h] = a
        w = weight_ref[:, cut(h)]
        inv = lax.rsqrt(jnp.mean(a * a, axis=1, keepdims=True) + EPSILON)
        partial = partial + jnp.sum(a * w, axis=1, keepdims=True) * inv

    part_row = jnp.sum(jnp.where(eye, partial, 0.0), axis=0, keepdims=True)
    vals[head] = jnp.broadcast_to(part_row, (8, T))

    def value_copy(slot, to):
        return pltpu.make_async_remote_copy(
            src_ref=vals.at[slot], dst_ref=vals.at[slot], send_sem=v_send.at[to],
            recv_sem=v_recv.at[slot], device_id={"head": to}, device_id_type=MESH,
        )

    for o in range(1, n_head):
        value_copy(head, lax.rem(head + o, n_head)).start()
    for o in range(1, n_head):
        value_copy(lax.rem(head + o, n_head), lax.rem(head + o, n_head)).wait_recv()
    value_row = vals[0, 0:1, :]
    for o in range(1, n_head):
        value_row = value_row + vals[o, 0:1, :]
    value_out[...] = value_row
    res_row = value_row - target_ref[...]
    res = jnp.sum(jnp.where(eye, res_row, 0.0), axis=1, keepdims=True)

    for h in range(heads):
        a = att[h]
        w = weight_ref[:, cut(h)]
        inv = lax.rsqrt(jnp.mean(a * a, axis=1, keepdims=True) + EPSILON)
        aw = jnp.mean(a * w, axis=1, keepdims=True)
        ri = res * inv
        red[me, heads + h : heads + h + 1, :] = jnp.sum(a * ri, axis=0, keepdims=True)
        g = ri * (w - a * (inv * inv * aw))
        ga = (g * alive).astype(bf16)
        g_dir[h] = dot(ga, qd[h], 0, 0)
        if n_ctx > 1:
            @pl.when(ctx == n_ctx - 1)
            def _():
                grad_copy(h).start()
        att[h] = g
    if n_ctx == 1:
        g_in[...] = jnp.zeros_like(g_in)
    else:
        @pl.when(ctx == n_ctx - 1)
        def _():
            g_in[...] = jnp.zeros_like(g_in)

    for h in range(heads):
        g = att[h]
        gb = g.astype(bf16)
        ga = (g * alive).astype(bf16)
        dp = jnp.where(live, dot(gb, v_ref[0, :, cut(h)], 1, 1), 0.0).astype(bf16)
        dq_dec = dot(dp, kd[h], 1, 0) + dot(ga, s_in[h].astype(bf16), 1, 0)
        dq_out[0, :, cut(h)] = (dq_dec * e_up[h]).astype(bf16)
        dqd[h] = dq_dec * qd[h].astype(f32)
        dkd[h] = dot(dp, qd[h], 0, 0)
        ptg[h] = dot(probs[h], gb, 0, 0)

    upper_b = jnp.where(rows <= cols, 1.0, 0.0).astype(bf16)
    for h in range(heads):
        if n_ctx > 1:
            @pl.when(ctx < n_ctx - 1)
            def _():
                grad_copy(h).wait_recv()

            @pl.when((ctx > 0) & (ctx < n_ctx - 1))
            def _():
                g_dir[h] = g_in[h] * (last[h : h + 1, :] * alive_last) + g_dir[h]
                grad_copy(h).start()

        up_last = last[h : h + 1, :]
        gs = g_in[h]
        gsb = gs.astype(bf16)
        dv_out[0, :, cut(h)] = (ptg[h] + dot(kt[h], gsb, 1, 1)).astype(bf16)
        tk = dot(vt[h], gsb, 1, 0) * up_last
        k_dec = kd[h].astype(f32)
        dk_dec = dkd[h] + tk
        dk_out[0, :, cut(h)] = (dk_dec * e_down[h]).astype(bf16)
        d_last = jnp.sum(k_dec * tk, axis=0, keepdims=True) + (
            jnp.sum(s_in[h] * gs, axis=0, keepdims=True) * (up_last * alive_last)
        )
        d_cum = dqd[h] - k_dec * dk_dec
        dx = (split_dot(upper_b, d_cum) + d_last) * slope[h]
        dg_out[0, :, cut(h)] = dx.astype(bf16)
        red[me, h : h + 1, :] = jnp.sum(dx, axis=0, keepdims=True)

    def red_copy(slot, to):
        return pltpu.make_async_remote_copy(
            src_ref=red.at[slot], dst_ref=red.at[slot], send_sem=r_send.at[to],
            recv_sem=r_recv.at[slot],
            device_id={"ctx": to // n_rep, "rep": lax.rem(to, n_rep)}, device_id_type=MESH,
        )

    for o in range(1, n_red):
        red_copy(me, lax.rem(me + o, n_red)).start()
    for o in range(1, n_red):
        other = lax.rem(me + o, n_red)
        red_copy(other, other).wait_recv()
    total = red[0]
    for o in range(1, n_red):
        total = total + red[o]
    total = total * (1.0 / (T * n_red))
    for h in range(heads):
        dbias_out[:, cut(h)] = total[h : h + 1, :]
        dweight_out[:, cut(h)] = total[heads + h : heads + h + 1, :]

    for o in range(1, n_red):
        red_copy(me, lax.rem(me + o, n_red)).wait_send()
    for o in range(1, n_head):
        value_copy(head, lax.rem(head + o, n_head)).wait_send()
    if n_ctx > 1:
        for h in range(heads):
            @pl.when(ctx < n_ctx - 1)
            def _():
                state_copy(h).wait_send()

            @pl.when(ctx > 0)
            def _():
                grad_copy(h).wait_send()


def on_device(n_ctx, n_head, n_rep, *args):
    q, k, v, g, bias, weight, targets, kinds, starts = args
    T, width = q.shape[1], q.shape[2]
    heads = width // DK
    n_red = n_ctx * n_rep
    vm = pl.BlockSpec(memory_space=pltpu.VMEM)
    half = lambda: pltpu.VMEM((heads, T, DK), bf16)
    full = lambda: pltpu.VMEM((heads, T, DK), f32)
    sems = lambda n: pltpu.SemaphoreType.DMA((n,))
    row16 = jax.ShapeDtypeStruct((1, T, width), bf16)
    row = jax.ShapeDtypeStruct((1, width), f32)
    outs = pl.pallas_call(
        functools.partial(kernel, n_ctx, n_head, n_rep, heads),
        out_shape=(jax.ShapeDtypeStruct((1, T), f32), row16, row16, row16, row16, row, row),
        in_specs=[vm] * 9,
        out_specs=(vm,) * 7,
        scratch_shapes=[
            half(), half(), half(), half(), pltpu.VMEM((heads, T, T), bf16),
            full(), full(), full(), full(), full(), full(), full(), full(),
            full(), full(), full(), pltpu.VMEM((8, DK), f32),
            pltpu.VMEM((n_head, 8, T), f32), pltpu.VMEM((n_red, 2 * heads, DK), f32),
            sems(heads), sems(heads), sems(heads), sems(heads),
            sems(n_head), sems(n_head), sems(n_red), sems(n_red),
        ],
        compiler_params=pltpu.CompilerParams(
            collective_id=0, has_side_effects=True, vmem_limit_bytes=24 * 2**20
        ),
    )(q, k, v, g, bias.reshape(1, width), weight.reshape(1, width), targets, kinds, starts)
    value, dq, dk, dv, dg, dbias, dweight = outs
    return value, dq, dk, dv, dg, dbias.reshape(width), dweight.reshape(width)


def solution(mesh):
    rows = ("groups", "rep")
    full, tokens = P(rows, "ctx", "head"), P(rows, "ctx")
    sums = P(("groups", "head"))
    shape = mesh.shape
    return jax.shard_map(
        functools.partial(on_device, shape["ctx"], shape["head"], shape["rep"]),
        mesh=mesh,
        in_specs=(full, full, full, full, P("head"), P("head"), tokens, tokens, tokens),
        out_specs=(tokens, full, full, full, full, sums, sums),
        check_vma=False,
    )
```

```python
import functools

import jax
import jax.numpy as jnp
from jax import lax
from jax.experimental import pallas as pl
from jax.experimental.pallas import tpu as pltpu
from jax.sharding import PartitionSpec as P

DK = 128
DV = 128
CUTS = 2
ROWS = DV // CUTS
EPSILON = 1.0
GATE_SCALE = 16.0
MESH = pl.DeviceIdType.MESH
f32 = jnp.float32
bf16 = jnp.bfloat16


def dot(a, b, da, db):
    return lax.dot_general(a, b, (((da,), (db,)), ((), ())), preferred_element_type=f32)


def split_dot(ones, x):
    hi = x.astype(bf16)
    lo = (x - hi.astype(f32)).astype(bf16)
    return dot(ones, hi, 1, 0) + dot(ones, lo, 1, 0)


def kernel(
    n_ctx, n_head, n_rep, heads,
    q_hbm, k_hbm, v_hbm, g_hbm, bias_hbm, weight_hbm, target_hbm, kind_hbm, start_hbm,
    value_hbm, dq_hbm, dk_hbm, dv_hbm, dg_hbm, dbias_hbm, dweight_hbm,
    q_ref, k_ref, v_ref, g_ref, bias_ref, weight_ref, target_ref, kind_ref, start_ref, loaded,
    qd, kd, kt, vt, probs, e_up, e_down, slope, att, s_loc, s_pair, s_in, g_dir, g_pair, g_in,
    ptg, dqd, dkd, last, pass_on, pair_pass, vals, red, dq_ref, dk_ref, dv_ref, dg_ref, rows_ref,
    s_send, s_far, sp_recv, s_recv, g_send, g_far, gp_recv, g_recv, d_send, d_recv,
    v_send, v_recv, r_send, r_recv, stored,
):
    T = q_ref.shape[1]
    loads = {
        name: pltpu.make_async_copy(src, dst, loaded.at[i])
        for i, (name, src, dst) in enumerate((
            ("gates", g_hbm, g_ref), ("bias", bias_hbm, bias_ref), ("starts", start_hbm, start_ref),
            ("keys", k_hbm, k_ref), ("values", v_hbm, v_ref), ("queries", q_hbm, q_ref),
            ("kinds", kind_hbm, kind_ref), ("weights", weight_hbm, weight_ref),
            ("targets", target_hbm, target_ref),
        ))
    }
    for load in loads.values():
        load.start()
    ctx = lax.axis_index("ctx")
    head = lax.axis_index("head")
    rep = lax.axis_index("rep")
    n_red = n_ctx * n_rep
    me = ctx * n_rep + rep

    barrier = pltpu.get_barrier_semaphore()
    for o in range(1, n_red):
        to = lax.rem(me + o, n_red)
        pl.semaphore_signal(
            barrier, inc=1, device_id={"ctx": to // n_rep, "rep": lax.rem(to, n_rep)},
            device_id_type=MESH,
        )
    for o in range(1, n_head):
        pl.semaphore_signal(
            barrier, inc=1, device_id={"head": lax.rem(head + o, n_head)}, device_id_type=MESH
        )

    rows = lax.broadcasted_iota(jnp.int32, (T, T), 0)
    cols = lax.broadcasted_iota(jnp.int32, (T, T), 1)
    lower = (rows >= cols)
    lower_b = jnp.where(lower, 1.0, 0.0).astype(bf16)
    loads["starts"].wait()
    flags = start_ref[...].astype(f32)
    seg_col = jnp.sum(jnp.where(lower, flags, 0.0), axis=1, keepdims=True)
    seg_last = jnp.sum(flags, axis=1, keepdims=True)
    alive = jnp.where(seg_col == 0.0, 1.0, 0.0)
    tail = jnp.where(seg_col == seg_last, 1.0, 0.0)
    alive_last = jnp.where(seg_last == 0.0, 1.0, 0.0)

    def cut(h):
        return slice(h * DK, (h + 1) * DK)

    pair, odd = ctx // 2, lax.rem(ctx, 2)
    pairs = n_ctx // 2
    first, final = pair == 0, pair == pairs - 1

    def piece(ref, c):
        return ref.at[c // CUTS, pl.ds(c % CUTS * ROWS, ROWS)]

    def move(src, dst, c, send, recv, by):
        return pltpu.make_async_remote_copy(
            src_ref=piece(src, c), dst_ref=piece(dst, c), send_sem=send.at[c], recv_sem=recv.at[c],
            device_id={"ctx": lax.rem(ctx + by + n_ctx, n_ctx)}, device_id_type=MESH,
        )

    def state_to_pair(c):
        return move(s_loc, s_pair, c, s_send, sp_recv, 1)

    def state_near(c):
        return move(s_loc, s_in, c, s_send, s_recv, 1)

    def state_far(c):
        return move(s_loc, s_in, c, s_far, s_recv, 2)

    def grad_to_pair(c):
        return move(g_dir, g_pair, c, g_send, gp_recv, -1)

    def grad_near(c):
        return move(g_dir, g_in, c, g_send, g_recv, -1)

    def grad_far(c):
        return move(g_dir, g_in, c, g_far, g_recv, -2)

    def of_head(h):
        return range(h * CUTS, (h + 1) * CUTS)

    pieces = range(heads * CUTS)
    pass_copy = pltpu.make_async_remote_copy(
        src_ref=pass_on, dst_ref=pair_pass, send_sem=d_send.at[0], recv_sem=d_recv.at[0],
        device_id={"ctx": ctx + 1 - 2 * odd}, device_id_type=MESH,
    )

    def store(i, src, dst):
        return pltpu.make_async_copy(src, dst, stored.at[i])

    pass_on[...] = jnp.zeros_like(pass_on)
    for name in ("gates", "bias", "keys", "values"):
        loads[name].wait()
    for h in range(heads):
        x = g_ref[0, :, cut(h)].astype(f32) + bias_ref[:, cut(h)]
        e = jnp.exp(-jnp.abs(x))
        decay = (jnp.minimum(x, 0.0) - jnp.log(1.0 + e)) * (1.0 / GATE_SCALE)
        slope[h] = jnp.where(x >= 0.0, e, 1.0) / (1.0 + e) * (1.0 / GATE_SCALE)
        cum = split_dot(lower_b, decay)
        up = jnp.exp(cum)
        down = jnp.exp(-cum)
        e_up[h] = up * DK ** (-0.5)
        e_down[h] = down
        up_last = up[T - 1 : T, :]
        last[h : h + 1, :] = up_last
        pass_on[h : h + 1, :] = up_last * alive_last
        k_dec = k_ref[0, :, cut(h)].astype(f32) * down
        kd[h] = k_dec.astype(bf16)
        tail_k = (k_dec * up_last * tail).astype(bf16)
        kt[h] = tail_k
        s_loc[h] = dot(v_ref[0, :, cut(h)], tail_k, 0, 0)

    pl.semaphore_wait(barrier, n_red + n_head - 2)

    @pl.when(odd == 0)
    def _():
        for c in pieces:
            state_to_pair(c).start()

    @pl.when(ctx == 0)
    def _():
        s_in[...] = jnp.zeros_like(s_in)

    pass_copy.start()

    for name in ("queries", "kinds", "weights", "targets"):
        loads[name].wait()
    eye = rows == cols
    start_col = jnp.sum(jnp.where(eye, flags, 0.0), axis=1, keepdims=True)
    seg_row = jnp.sum(jnp.where(rows <= cols, start_col, 0.0), axis=0, keepdims=True)
    kind = kind_ref[...]
    window = jnp.where(kind == 0, T, jnp.where(kind == 1, T // 2, jnp.where(kind == 2, T // 4, T // 8)))
    live = lower & (seg_col == seg_row) & (rows - cols < window)
    for h in range(heads):
        q_dec = (q_ref[0, :, cut(h)].astype(f32) * e_up[h]).astype(bf16)
        qd[h] = q_dec
        p = jnp.where(live, dot(q_dec, kd[h], 1, 1), 0.0).astype(bf16)
        probs[h] = p
        att[h] = dot(p, v_ref[0, :, cut(h)], 1, 0)
        vt[h] = (v_ref[0, :, cut(h)].astype(f32) * tail).astype(bf16)

    partial = jnp.zeros((T, 1), f32)
    pass_copy.wait_recv()
    for h in range(heads):
        for c in of_head(h):
            part = (h, slice(c % CUTS * ROWS, (c % CUTS + 1) * ROWS))

            @pl.when((odd == 0) & ~first)
            def _():
                state_near(c).wait_recv()

            @pl.when((odd == 1) & first)
            def _():
                state_to_pair(c).wait_recv()
                s_in[part] = s_pair[part]

            @pl.when((odd == 1) & ~first)
            def _():
                state_to_pair(c).wait_recv()
                state_far(c).wait_recv()
                s_in[part] = s_in[part] * pair_pass[h : h + 1, :] + s_pair[part]

            @pl.when((odd == 1) & ~final)
            def _():
                s_loc[part] = s_in[part] * pass_on[h : h + 1, :] + s_loc[part]
                state_far(c).start()

        if h == heads - 1:
            @pl.when((odd == 1) & ~final)
            def _():
                for c in pieces:
                    state_near(c).start()

        a = att[h] + dot(qd[h], s_in[h].astype(bf16), 1, 1) * alive
        att[h] = a
        w = weight_ref[:, cut(h)]
        inv = lax.rsqrt(jnp.mean(a * a, axis=1, keepdims=True) + EPSILON)
        partial = partial + jnp.sum(a * w, axis=1, keepdims=True) * inv

    part_row = jnp.sum(jnp.where(eye, partial, 0.0), axis=0, keepdims=True)
    vals[head] = jnp.broadcast_to(part_row, (8, T))

    def value_copy(slot, to):
        return pltpu.make_async_remote_copy(
            src_ref=vals.at[slot], dst_ref=vals.at[slot], send_sem=v_send.at[to],
            recv_sem=v_recv.at[slot], device_id={"head": to}, device_id_type=MESH,
        )

    for o in range(1, n_head):
        value_copy(head, lax.rem(head + o, n_head)).start()
    for o in range(1, n_head):
        value_copy(lax.rem(head + o, n_head), lax.rem(head + o, n_head)).wait_recv()
    value_row = vals[0, 0:1, :]
    for o in range(1, n_head):
        value_row = value_row + vals[o, 0:1, :]
    rows_ref[0, :, 0:T] = value_row
    value_store = store(0, rows_ref.at[0, :, pl.ds(0, T)], value_hbm)
    value_store.start()
    res_row = value_row - target_ref[...]
    res = jnp.sum(jnp.where(eye, res_row, 0.0), axis=1, keepdims=True)

    for h in range(heads):
        a = att[h]
        w = weight_ref[:, cut(h)]
        inv = lax.rsqrt(jnp.mean(a * a, axis=1, keepdims=True) + EPSILON)
        aw = jnp.mean(a * w, axis=1, keepdims=True)
        ri = res * inv
        red[me, heads + h : heads + h + 1, :] = jnp.sum(a * ri, axis=0, keepdims=True)
        g = ri * (w - a * (inv * inv * aw))
        ga = (g * alive).astype(bf16)
        g_dir[h] = dot(ga, qd[h], 0, 0)
        @pl.when(odd == 1)
        def _():
            for c in of_head(h):
                grad_to_pair(c).start()

        att[h] = g

    @pl.when(ctx == n_ctx - 1)
    def _():
        g_in[...] = jnp.zeros_like(g_in)

    for h in range(heads):
        g = att[h]
        gb = g.astype(bf16)
        ga = (g * alive).astype(bf16)
        dp = jnp.where(live, dot(gb, v_ref[0, :, cut(h)], 1, 1), 0.0).astype(bf16)
        dq_dec = dot(dp, kd[h], 1, 0) + dot(ga, s_in[h].astype(bf16), 1, 0)
        dq_ref[0, :, cut(h)] = (dq_dec * e_up[h]).astype(bf16)
        dqd[h] = dq_dec * qd[h].astype(f32)
        dkd[h] = dot(dp, qd[h], 0, 0)
        ptg[h] = dot(probs[h], gb, 0, 0)

    stores = [value_store, store(1, dq_ref, dq_hbm)]
    stores[1].start()

    upper_b = jnp.where(rows <= cols, 1.0, 0.0).astype(bf16)
    for h in range(heads):
        for c in of_head(h):
            part = (h, slice(c % CUTS * ROWS, (c % CUTS + 1) * ROWS))

            @pl.when((odd == 1) & ~final)
            def _():
                grad_near(c).wait_recv()

            @pl.when((odd == 0) & final)
            def _():
                grad_to_pair(c).wait_recv()
                g_in[part] = g_pair[part]

            @pl.when((odd == 0) & ~final)
            def _():
                grad_to_pair(c).wait_recv()
                grad_far(c).wait_recv()
                g_in[part] = g_in[part] * pair_pass[h : h + 1, :] + g_pair[part]

            @pl.when((odd == 0) & ~first)
            def _():
                g_dir[part] = g_in[part] * pass_on[h : h + 1, :] + g_dir[part]
                grad_far(c).start()

        if h == heads - 1:
            @pl.when((odd == 0) & ~first)
            def _():
                for c in pieces:
                    grad_near(c).start()

        up_last = last[h : h + 1, :]
        gs = g_in[h]
        gsb = gs.astype(bf16)
        dv_ref[0, :, cut(h)] = (ptg[h] + dot(kt[h], gsb, 1, 1)).astype(bf16)
        tk = dot(vt[h], gsb, 1, 0) * up_last
        k_dec = kd[h].astype(f32)
        dk_dec = dkd[h] + tk
        dk_ref[0, :, cut(h)] = (dk_dec * e_down[h]).astype(bf16)
        d_last = jnp.sum(k_dec * tk, axis=0, keepdims=True) + (
            jnp.sum(s_in[h] * gs, axis=0, keepdims=True) * (up_last * alive_last)
        )
        d_cum = dqd[h] - k_dec * dk_dec
        dx = (split_dot(upper_b, d_cum) + d_last) * slope[h]
        dg_ref[0, :, cut(h)] = dx.astype(bf16)
        red[me, h : h + 1, :] = jnp.sum(dx, axis=0, keepdims=True)

    for i, src, dst in ((2, dk_ref, dk_hbm), (3, dv_ref, dv_hbm), (4, dg_ref, dg_hbm)):
        stores.append(store(i, src, dst))
        stores[-1].start()

    def red_copy(slot, to):
        return pltpu.make_async_remote_copy(
            src_ref=red.at[slot], dst_ref=red.at[slot], send_sem=r_send.at[to],
            recv_sem=r_recv.at[slot],
            device_id={"ctx": to // n_rep, "rep": lax.rem(to, n_rep)}, device_id_type=MESH,
        )

    for o in range(1, n_red):
        red_copy(me, lax.rem(me + o, n_red)).start()
    for o in range(1, n_red):
        other = lax.rem(me + o, n_red)
        red_copy(other, other).wait_recv()
    total = red[0]
    for o in range(1, n_red):
        total = total + red[o]
    total = total * (1.0 / (T * n_red))
    for h in range(heads):
        rows_ref[1, :, cut(h)] = total[h : h + 1, :]
        rows_ref[2, :, cut(h)] = total[heads + h : heads + h + 1, :]

    for i, dst in ((5, dbias_hbm), (6, dweight_hbm)):
        stores.append(store(i, rows_ref.at[i - 4], dst))
        stores[-1].start()

    for o in range(1, n_red):
        red_copy(me, lax.rem(me + o, n_red)).wait_send()
    for o in range(1, n_head):
        value_copy(head, lax.rem(head + o, n_head)).wait_send()
    pass_copy.wait_send()

    @pl.when((odd == 0) | ~final)
    def _():
        for c in pieces:
            state_near(c).wait_send()

    @pl.when((odd == 1) & ~final)
    def _():
        for c in pieces:
            state_far(c).wait_send()

    @pl.when((odd == 1) | ~first)
    def _():
        for c in pieces:
            grad_near(c).wait_send()

    @pl.when((odd == 0) & ~first)
    def _():
        for c in pieces:
            grad_far(c).wait_send()

    for copy in stores:
        copy.wait()


def hand_on(*refs):
    count = len(refs) // 2
    copies = [
        pltpu.make_async_copy(refs[i], refs[count + i], refs[-1].at[i]) for i in range(count)
    ]
    for copy in copies:
        copy.start()
    for copy in copies:
        copy.wait()


def on_device(n_ctx, n_head, n_rep, *args):
    q, k, v, g, bias, weight, targets, kinds, starts = args
    T, width = q.shape[1], q.shape[2]
    heads = width // DK
    n_red = n_ctx * n_rep
    hbm = pl.BlockSpec(memory_space=pltpu.HBM)
    half = lambda: pltpu.VMEM((heads, T, DK), bf16)
    full = lambda: pltpu.VMEM((heads, T, DK), f32)
    sems = lambda n: pltpu.SemaphoreType.DMA((n,))
    row16 = jax.ShapeDtypeStruct((1, T, width), bf16)
    row = jax.ShapeDtypeStruct((1, width), f32)
    ins = (q, k, v, g, bias.reshape(1, width), weight.reshape(1, width), targets, kinds, starts)
    shapes = (jax.ShapeDtypeStruct((1, T), f32), row16, row16, row16, row16, row, row)
    outs = pl.pallas_call(
        functools.partial(kernel, n_ctx, n_head, n_rep, heads),
        out_shape=shapes,
        in_specs=[hbm] * 9,
        out_specs=(hbm,) * 7,
        scratch_shapes=[
            *(pltpu.VMEM(a.shape, a.dtype) for a in ins), sems(9),
            half(), half(), half(), half(), pltpu.VMEM((heads, T, T), bf16),
            *(full() for _ in range(13)), *(pltpu.VMEM((8, DK), f32) for _ in range(3)),
            pltpu.VMEM((n_head, 8, T), f32), pltpu.VMEM((n_red, 2 * heads, DK), f32),
            *(pltpu.VMEM((1, T, width), bf16) for _ in range(4)), pltpu.VMEM((3, 1, width), f32),
            *(sems(heads * CUTS) for _ in range(8)), sems(1), sems(1),
            sems(n_head), sems(n_head), sems(n_red), sems(n_red), sems(7),
        ],
        compiler_params=pltpu.CompilerParams(
            collective_id=0, has_side_effects=True, vmem_limit_bytes=60 * 2**20
        ),
    )(*ins)
    outs = pl.pallas_call(
        hand_on,
        out_shape=shapes,
        in_specs=[hbm] * 7,
        out_specs=(hbm,) * 7,
        scratch_shapes=[sems(7)],
        compiler_params=pltpu.CompilerParams(vmem_limit_bytes=60 * 2**20),
    )(*outs)
    value, dq, dk, dv, dg, dbias, dweight = outs
    return value, dq, dk, dv, dg, dbias.reshape(width), dweight.reshape(width)


def solution(mesh):
    rows = ("groups", "rep")
    full, tokens = P(rows, "ctx", "head"), P(rows, "ctx")
    sums = P(("groups", "head"))
    shape = mesh.shape
    return jax.shard_map(
        functools.partial(on_device, shape["ctx"], shape["head"], shape["rep"]),
        mesh=mesh,
        in_specs=(full, full, full, full, P("head"), P("head"), tokens, tokens, tokens),
        out_specs=(tokens, full, full, full, full, sums, sums),
        check_vma=False,
    )
```

```python
import functools

import jax
import jax.numpy as jnp
from jax import lax
from jax.experimental import pallas as pl
from jax.experimental.pallas import tpu as pltpu
from jax.sharding import PartitionSpec as P

DK = 128
DV = 128
CUTS = 4
ROWS = DV // CUTS
EPSILON = 1.0
GATE_SCALE = 16.0
MESH = pl.DeviceIdType.MESH
f32 = jnp.float32
bf16 = jnp.bfloat16


def dot(a, b, da, db):
    return lax.dot_general(a, b, (((da,), (db,)), ((), ())), preferred_element_type=f32)


def split_dot(ones, x):
    hi = x.astype(bf16)
    lo = (x - hi.astype(f32)).astype(bf16)
    return dot(ones, hi, 1, 0) + dot(ones, lo, 1, 0)


def kernel(
    n_ctx, n_head, n_rep, heads,
    q_hbm, k_hbm, v_hbm, g_hbm, bias_hbm, weight_hbm, target_hbm, kind_hbm, start_hbm,
    value_out, dq_out, dk_out, dv_out, dg_out, dbias_out, dweight_out,
    q_ref, k_ref, v_ref, g_ref, bias_ref, weight_ref, target_ref, kind_ref, start_ref, loaded,
    qd, kd, kt, vt, probs, e_up, e_down, slope, att, s_loc, s_in, g_dir, g_in,
    ptg, dqd, dkd, last, vals, red,
    s_send, s_recv, gs_send, gs_recv, v_send, v_recv, r_send, r_recv,
):
    T = q_ref.shape[1]
    loads = {
        name: pltpu.make_async_copy(src, dst, loaded.at[i])
        for i, (name, src, dst) in enumerate((
            ("gates", g_hbm, g_ref), ("bias", bias_hbm, bias_ref), ("starts", start_hbm, start_ref),
            ("keys", k_hbm, k_ref), ("values", v_hbm, v_ref), ("queries", q_hbm, q_ref),
            ("kinds", kind_hbm, kind_ref), ("weights", weight_hbm, weight_ref),
            ("targets", target_hbm, target_ref),
        ))
    }
    for load in loads.values():
        load.start()
    ctx = lax.axis_index("ctx")
    head = lax.axis_index("head")
    rep = lax.axis_index("rep")
    n_red = n_ctx * n_rep
    me = ctx * n_rep + rep

    barrier = pltpu.get_barrier_semaphore()
    for o in range(1, n_red):
        to = lax.rem(me + o, n_red)
        pl.semaphore_signal(
            barrier, inc=1, device_id={"ctx": to // n_rep, "rep": lax.rem(to, n_rep)},
            device_id_type=MESH,
        )
    for o in range(1, n_head):
        pl.semaphore_signal(
            barrier, inc=1, device_id={"head": lax.rem(head + o, n_head)}, device_id_type=MESH
        )

    rows = lax.broadcasted_iota(jnp.int32, (T, T), 0)
    cols = lax.broadcasted_iota(jnp.int32, (T, T), 1)
    lower = (rows >= cols)
    lower_b = jnp.where(lower, 1.0, 0.0).astype(bf16)
    loads["starts"].wait()
    flags = start_ref[...].astype(f32)
    seg_col = jnp.sum(jnp.where(lower, flags, 0.0), axis=1, keepdims=True)
    seg_last = jnp.sum(flags, axis=1, keepdims=True)
    alive = jnp.where(seg_col == 0.0, 1.0, 0.0)
    tail = jnp.where(seg_col == seg_last, 1.0, 0.0)
    alive_last = jnp.where(seg_last == 0.0, 1.0, 0.0)

    def cut(h):
        return slice(h * DK, (h + 1) * DK)

    def state_copy(h):
        return pltpu.make_async_remote_copy(
            src_ref=s_loc.at[h // CUTS, pl.ds(h % CUTS * ROWS, ROWS)], dst_ref=s_in.at[h // CUTS, pl.ds(h % CUTS * ROWS, ROWS)], send_sem=s_send.at[h], recv_sem=s_recv.at[h],
            device_id={"ctx": lax.rem(ctx + 1, n_ctx)}, device_id_type=MESH,
        )

    def grad_copy(h):
        return pltpu.make_async_remote_copy(
            src_ref=g_dir.at[h // CUTS, pl.ds(h % CUTS * ROWS, ROWS)], dst_ref=g_in.at[h // CUTS, pl.ds(h % CUTS * ROWS, ROWS)], send_sem=gs_send.at[h], recv_sem=gs_recv.at[h],
            device_id={"ctx": lax.rem(ctx + n_ctx - 1, n_ctx)}, device_id_type=MESH,
        )

    for name in ("gates", "bias", "keys", "values"):
        loads[name].wait()
    for h in range(heads):
        x = g_ref[0, :, cut(h)].astype(f32) + bias_ref[:, cut(h)]
        e = jnp.exp(-jnp.abs(x))
        decay = (jnp.minimum(x, 0.0) - jnp.log(1.0 + e)) * (1.0 / GATE_SCALE)
        slope[h] = jnp.where(x >= 0.0, e, 1.0) / (1.0 + e) * (1.0 / GATE_SCALE)
        cum = split_dot(lower_b, decay)
        up = jnp.exp(cum)
        down = jnp.exp(-cum)
        e_up[h] = up * DK ** (-0.5)
        e_down[h] = down
        up_last = up[T - 1 : T, :]
        last[h : h + 1, :] = up_last
        k_dec = k_ref[0, :, cut(h)].astype(f32) * down
        kd[h] = k_dec.astype(bf16)
        tail_k = (k_dec * up_last * tail).astype(bf16)
        kt[h] = tail_k
        s_loc[h] = dot(v_ref[0, :, cut(h)], tail_k, 0, 0)

    pl.semaphore_wait(barrier, n_red + n_head - 2)

    @pl.when(ctx == 0)
    def _():
        if n_ctx > 1:
            for c in range(CUTS * heads):
                state_copy(c).start()
        s_in[...] = jnp.zeros_like(s_in)

    for name in ("queries", "kinds", "weights", "targets"):
        loads[name].wait()
    eye = rows == cols
    start_col = jnp.sum(jnp.where(eye, flags, 0.0), axis=1, keepdims=True)
    seg_row = jnp.sum(jnp.where(rows <= cols, start_col, 0.0), axis=0, keepdims=True)
    kind = kind_ref[...]
    window = jnp.where(kind == 0, T, jnp.where(kind == 1, T // 2, jnp.where(kind == 2, T // 4, T // 8)))
    live = lower & (seg_col == seg_row) & (rows - cols < window)
    for h in range(heads):
        q_dec = (q_ref[0, :, cut(h)].astype(f32) * e_up[h]).astype(bf16)
        qd[h] = q_dec
        p = jnp.where(live, dot(q_dec, kd[h], 1, 1), 0.0).astype(bf16)
        probs[h] = p
        att[h] = dot(p, v_ref[0, :, cut(h)], 1, 0)
        vt[h] = (v_ref[0, :, cut(h)].astype(f32) * tail).astype(bf16)

    partial = jnp.zeros((T, 1), f32)
    for h in range(heads):
        if n_ctx > 1:
            for c in range(h * CUTS, (h + 1) * CUTS):
                part = (h, slice(c % CUTS * ROWS, (c % CUTS + 1) * ROWS))

                @pl.when(ctx > 0)
                def _():
                    state_copy(c).wait_recv()

                @pl.when((ctx > 0) & (ctx < n_ctx - 1))
                def _():
                    s_loc[part] = s_in[part] * (last[h : h + 1, :] * alive_last) + s_loc[part]
                    state_copy(c).start()

        a = att[h] + dot(qd[h], s_in[h].astype(bf16), 1, 1) * alive
        att[h] = a
        w = weight_ref[:, cut(h)]
        inv = lax.rsqrt(jnp.mean(a * a, axis=1, keepdims=True) + EPSILON)
        partial = partial + jnp.sum(a * w, axis=1, keepdims=True) * inv

    part_row = jnp.sum(jnp.where(eye, partial, 0.0), axis=0, keepdims=True)
    vals[head] = jnp.broadcast_to(part_row, (8, T))

    def value_copy(slot, to):
        return pltpu.make_async_remote_copy(
            src_ref=vals.at[slot], dst_ref=vals.at[slot], send_sem=v_send.at[to],
            recv_sem=v_recv.at[slot], device_id={"head": to}, device_id_type=MESH,
        )

    for o in range(1, n_head):
        value_copy(head, lax.rem(head + o, n_head)).start()
    for o in range(1, n_head):
        value_copy(lax.rem(head + o, n_head), lax.rem(head + o, n_head)).wait_recv()
    value_row = vals[0, 0:1, :]
    for o in range(1, n_head):
        value_row = value_row + vals[o, 0:1, :]
    value_out[...] = value_row
    res_row = value_row - target_ref[...]
    res = jnp.sum(jnp.where(eye, res_row, 0.0), axis=1, keepdims=True)

    for h in range(heads):
        a = att[h]
        w = weight_ref[:, cut(h)]
        inv = lax.rsqrt(jnp.mean(a * a, axis=1, keepdims=True) + EPSILON)
        aw = jnp.mean(a * w, axis=1, keepdims=True)
        ri = res * inv
        red[me, heads + h : heads + h + 1, :] = jnp.sum(a * ri, axis=0, keepdims=True)
        g = ri * (w - a * (inv * inv * aw))
        ga = (g * alive).astype(bf16)
        g_dir[h] = dot(ga, qd[h], 0, 0)
        if n_ctx > 1:
            @pl.when(ctx == n_ctx - 1)
            def _():
                for c in range(h * CUTS, (h + 1) * CUTS):
                    grad_copy(c).start()
        att[h] = g
    if n_ctx == 1:
        g_in[...] = jnp.zeros_like(g_in)
    else:
        @pl.when(ctx == n_ctx - 1)
        def _():
            g_in[...] = jnp.zeros_like(g_in)

    for h in range(heads):
        g = att[h]
        gb = g.astype(bf16)
        ga = (g * alive).astype(bf16)
        dp = jnp.where(live, dot(gb, v_ref[0, :, cut(h)], 1, 1), 0.0).astype(bf16)
        dq_dec = dot(dp, kd[h], 1, 0) + dot(ga, s_in[h].astype(bf16), 1, 0)
        dq_out[0, :, cut(h)] = (dq_dec * e_up[h]).astype(bf16)
        dqd[h] = dq_dec * qd[h].astype(f32)
        dkd[h] = dot(dp, qd[h], 0, 0)
        ptg[h] = dot(probs[h], gb, 0, 0)

    upper_b = jnp.where(rows <= cols, 1.0, 0.0).astype(bf16)
    for h in range(heads):
        if n_ctx > 1:
            for c in range(h * CUTS, (h + 1) * CUTS):
                part = (h, slice(c % CUTS * ROWS, (c % CUTS + 1) * ROWS))

                @pl.when(ctx < n_ctx - 1)
                def _():
                    grad_copy(c).wait_recv()

                @pl.when((ctx > 0) & (ctx < n_ctx - 1))
                def _():
                    g_dir[part] = g_in[part] * (last[h : h + 1, :] * alive_last) + g_dir[part]
                    grad_copy(c).start()

        up_last = last[h : h + 1, :]
        gs = g_in[h]
        gsb = gs.astype(bf16)
        dv_out[0, :, cut(h)] = (ptg[h] + dot(kt[h], gsb, 1, 1)).astype(bf16)
        tk = dot(vt[h], gsb, 1, 0) * up_last
        k_dec = kd[h].astype(f32)
        dk_dec = dkd[h] + tk
        dk_out[0, :, cut(h)] = (dk_dec * e_down[h]).astype(bf16)
        d_last = jnp.sum(k_dec * tk, axis=0, keepdims=True) + (
            jnp.sum(s_in[h] * gs, axis=0, keepdims=True) * (up_last * alive_last)
        )
        d_cum = dqd[h] - k_dec * dk_dec
        dx = (split_dot(upper_b, d_cum) + d_last) * slope[h]
        dg_out[0, :, cut(h)] = dx.astype(bf16)
        red[me, h : h + 1, :] = jnp.sum(dx, axis=0, keepdims=True)

    def red_copy(slot, to):
        return pltpu.make_async_remote_copy(
            src_ref=red.at[slot], dst_ref=red.at[slot], send_sem=r_send.at[to],
            recv_sem=r_recv.at[slot],
            device_id={"ctx": to // n_rep, "rep": lax.rem(to, n_rep)}, device_id_type=MESH,
        )

    for o in range(1, n_red):
        red_copy(me, lax.rem(me + o, n_red)).start()
    for o in range(1, n_red):
        other = lax.rem(me + o, n_red)
        red_copy(other, other).wait_recv()
    total = red[0]
    for o in range(1, n_red):
        total = total + red[o]
    total = total * (1.0 / (T * n_red))
    for h in range(heads):
        dbias_out[:, cut(h)] = total[h : h + 1, :]
        dweight_out[:, cut(h)] = total[heads + h : heads + h + 1, :]

    for o in range(1, n_red):
        red_copy(me, lax.rem(me + o, n_red)).wait_send()
    for o in range(1, n_head):
        value_copy(head, lax.rem(head + o, n_head)).wait_send()
    if n_ctx > 1:
        for h in range(CUTS * heads):
            @pl.when(ctx < n_ctx - 1)
            def _():
                state_copy(h).wait_send()

            @pl.when(ctx > 0)
            def _():
                grad_copy(h).wait_send()


def on_device(n_ctx, n_head, n_rep, *args):
    q, k, v, g, bias, weight, targets, kinds, starts = args
    T, width = q.shape[1], q.shape[2]
    heads = width // DK
    n_red = n_ctx * n_rep
    vm = pl.BlockSpec(memory_space=pltpu.VMEM)
    hbm = pl.BlockSpec(memory_space=pltpu.HBM)
    half = lambda: pltpu.VMEM((heads, T, DK), bf16)
    full = lambda: pltpu.VMEM((heads, T, DK), f32)
    sems = lambda n: pltpu.SemaphoreType.DMA((n,))
    row16 = jax.ShapeDtypeStruct((1, T, width), bf16)
    row = jax.ShapeDtypeStruct((1, width), f32)
    ins = (q, k, v, g, bias.reshape(1, width), weight.reshape(1, width), targets, kinds, starts)
    shapes = (jax.ShapeDtypeStruct((1, T), f32), row16, row16, row16, row16, row, row)
    outs = pl.pallas_call(
        functools.partial(kernel, n_ctx, n_head, n_rep, heads),
        out_shape=shapes,
        in_specs=[hbm] * 9,
        out_specs=(vm,) * 7,
        scratch_shapes=[
            *(pltpu.VMEM(a.shape, a.dtype) for a in ins), sems(9),
            half(), half(), half(), half(), pltpu.VMEM((heads, T, T), bf16),
            full(), full(), full(), full(), full(), full(), full(), full(),
            full(), full(), full(), pltpu.VMEM((8, DK), f32),
            pltpu.VMEM((n_head, 8, T), f32), pltpu.VMEM((n_red, 2 * heads, DK), f32),
            *(sems(CUTS * heads) for _ in range(4)),
            sems(n_head), sems(n_head), sems(n_red), sems(n_red),
        ],
        compiler_params=pltpu.CompilerParams(
            collective_id=0, has_side_effects=True, vmem_limit_bytes=60 * 2**20
        ),
    )(*ins)
    value, dq, dk, dv, dg, dbias, dweight = outs
    return value, dq, dk, dv, dg, dbias.reshape(width), dweight.reshape(width)


def solution(mesh):
    rows = ("groups", "rep")
    full, tokens = P(rows, "ctx", "head"), P(rows, "ctx")
    sums = P(("groups", "head"))
    shape = mesh.shape
    return jax.shard_map(
        functools.partial(on_device, shape["ctx"], shape["head"], shape["rep"]),
        mesh=mesh,
        in_specs=(full, full, full, full, P("head"), P("head"), tokens, tokens, tokens),
        out_specs=(tokens, full, full, full, full, sums, sums),
        check_vma=False,
    )
```

```python
import functools

import jax
import jax.numpy as jnp
from jax import lax
from jax.experimental import pallas as pl
from jax.experimental.pallas import tpu as pltpu
from jax.sharding import PartitionSpec as P

DK = 128
DV = 128
CUTS = 4
ROWS = DV // CUTS
EPSILON = 1.0
GATE_SCALE = 16.0
MESH = pl.DeviceIdType.MESH
f32 = jnp.float32
bf16 = jnp.bfloat16


def dot(a, b, da, db):
    return lax.dot_general(a, b, (((da,), (db,)), ((), ())), preferred_element_type=f32)


def split_dot(ones, x):
    hi = x.astype(bf16)
    lo = (x - hi.astype(f32)).astype(bf16)
    return dot(ones, hi, 1, 0) + dot(ones, lo, 1, 0)


def kernel(
    n_ctx, n_head, n_rep, heads,
    q_hbm, k_hbm, v_hbm, g_hbm, bias_hbm, weight_hbm, target_hbm, kind_hbm, start_hbm,
    value_out, dq_out, dk_out, dv_out, dg_out, dbias_out, dweight_out,
    q_ref, k_ref, v_ref, g_ref, bias_ref, weight_ref, target_ref, kind_ref, start_ref, loaded,
    qd, kd, kt, vt, probs, e_up, e_down, slope, att, s_loc, s_in, g_dir, g_in,
    ptg, dqd, dkd, last, vals, red,
    s_send, s_recv, gs_send, gs_recv, v_send, v_recv, r_send, r_recv,
):
    T = q_ref.shape[1]
    loads = {
        name: pltpu.make_async_copy(src, dst, loaded.at[i])
        for i, (name, src, dst) in enumerate((
            ("gates", g_hbm, g_ref), ("bias", bias_hbm, bias_ref), ("starts", start_hbm, start_ref),
            ("keys", k_hbm, k_ref), ("values", v_hbm, v_ref), ("queries", q_hbm, q_ref),
            ("kinds", kind_hbm, kind_ref), ("weights", weight_hbm, weight_ref),
            ("targets", target_hbm, target_ref),
        ))
    }
    for load in loads.values():
        load.start()
    ctx = lax.axis_index("ctx")
    head = lax.axis_index("head")
    rep = lax.axis_index("rep")
    n_red = n_ctx * n_rep
    me = ctx * n_rep + rep

    barrier = pltpu.get_barrier_semaphore()
    for o in range(1, n_red):
        to = lax.rem(me + o, n_red)
        pl.semaphore_signal(
            barrier, inc=1, device_id={"ctx": to // n_rep, "rep": lax.rem(to, n_rep)},
            device_id_type=MESH,
        )
    for o in range(1, n_head):
        pl.semaphore_signal(
            barrier, inc=1, device_id={"head": lax.rem(head + o, n_head)}, device_id_type=MESH
        )

    rows = lax.broadcasted_iota(jnp.int32, (T, T), 0)
    cols = lax.broadcasted_iota(jnp.int32, (T, T), 1)
    lower = (rows >= cols)
    lower_b = jnp.where(lower, 1.0, 0.0).astype(bf16)
    loads["starts"].wait()
    flags = start_ref[...].astype(f32)
    seg_col = jnp.sum(jnp.where(lower, flags, 0.0), axis=1, keepdims=True)
    seg_last = jnp.sum(flags, axis=1, keepdims=True)
    alive = jnp.where(seg_col == 0.0, 1.0, 0.0)
    tail = jnp.where(seg_col == seg_last, 1.0, 0.0)
    alive_last = jnp.where(seg_last == 0.0, 1.0, 0.0)

    def cut(h):
        return slice(h * DK, (h + 1) * DK)

    def state_copy(h):
        return pltpu.make_async_remote_copy(
            src_ref=s_loc.at[h // CUTS, pl.ds(h % CUTS * ROWS, ROWS)], dst_ref=s_in.at[h // CUTS, pl.ds(h % CUTS * ROWS, ROWS)], send_sem=s_send.at[h], recv_sem=s_recv.at[h],
            device_id={"ctx": lax.rem(ctx + 1, n_ctx)}, device_id_type=MESH,
        )

    def grad_copy(h):
        return pltpu.make_async_remote_copy(
            src_ref=g_dir.at[h // CUTS, pl.ds(h % CUTS * ROWS, ROWS)], dst_ref=g_in.at[h // CUTS, pl.ds(h % CUTS * ROWS, ROWS)], send_sem=gs_send.at[h], recv_sem=gs_recv.at[h],
            device_id={"ctx": lax.rem(ctx + n_ctx - 1, n_ctx)}, device_id_type=MESH,
        )

    for name in ("gates", "bias", "keys", "values"):
        loads[name].wait()
    for h in range(heads):
        x = g_ref[0, :, cut(h)].astype(f32) + bias_ref[:, cut(h)]
        e = jnp.exp(-jnp.abs(x))
        decay = (jnp.minimum(x, 0.0) - jnp.log(1.0 + e)) * (1.0 / GATE_SCALE)
        slope[h] = jnp.where(x >= 0.0, e, 1.0) / (1.0 + e) * (1.0 / GATE_SCALE)
        cum = split_dot(lower_b, decay)
        up = jnp.exp(cum)
        down = jnp.exp(-cum)
        e_up[h] = up * DK ** (-0.5)
        e_down[h] = down
        up_last = up[T - 1 : T, :]
        last[h : h + 1, :] = up_last
        k_dec = k_ref[0, :, cut(h)].astype(f32) * down
        kd[h] = k_dec.astype(bf16)
        tail_k = (k_dec * up_last * tail).astype(bf16)
        kt[h] = tail_k
        s_loc[h] = dot(v_ref[0, :, cut(h)], tail_k, 0, 0)

    pl.semaphore_wait(barrier, n_red + n_head - 2)

    @pl.when(ctx == 0)
    def _():
        if n_ctx > 1:
            for c in range(CUTS * heads):
                state_copy(c).start()
        s_in[...] = jnp.zeros_like(s_in)

    for name in ("queries", "kinds", "weights", "targets"):
        loads[name].wait()
    eye = rows == cols
    start_col = jnp.sum(jnp.where(eye, flags, 0.0), axis=1, keepdims=True)
    seg_row = jnp.sum(jnp.where(rows <= cols, start_col, 0.0), axis=0, keepdims=True)
    kind = kind_ref[...]
    window = jnp.where(kind == 0, T, jnp.where(kind == 1, T // 2, jnp.where(kind == 2, T // 4, T // 8)))
    live = lower & (seg_col == seg_row) & (rows - cols < window)
    for h in range(heads):
        q_dec = (q_ref[0, :, cut(h)].astype(f32) * e_up[h]).astype(bf16)
        qd[h] = q_dec
        p = jnp.where(live, dot(q_dec, kd[h], 1, 1), 0.0).astype(bf16)
        probs[h] = p
        att[h] = dot(p, v_ref[0, :, cut(h)], 1, 0)
        vt[h] = (v_ref[0, :, cut(h)].astype(f32) * tail).astype(bf16)

    partial = jnp.zeros((T, 1), f32)
    for h in range(heads):
        if n_ctx > 1:
            for c in range(h * CUTS, (h + 1) * CUTS):
                part = (h, slice(c % CUTS * ROWS, (c % CUTS + 1) * ROWS))

                @pl.when(ctx > 0)
                def _():
                    state_copy(c).wait_recv()

                @pl.when((ctx > 0) & (ctx < n_ctx - 1))
                def _():
                    s_loc[part] = s_in[part] * (last[h : h + 1, :] * alive_last) + s_loc[part]
                    state_copy(c).start()

        a = att[h] + dot(qd[h], s_in[h].astype(bf16), 1, 1) * alive
        att[h] = a
        w = weight_ref[:, cut(h)]
        inv = lax.rsqrt(jnp.mean(a * a, axis=1, keepdims=True) + EPSILON)
        partial = partial + jnp.sum(a * w, axis=1, keepdims=True) * inv

    part_row = jnp.sum(jnp.where(eye, partial, 0.0), axis=0, keepdims=True)
    vals[head] = jnp.broadcast_to(part_row, (8, T))

    def value_copy(slot, to):
        return pltpu.make_async_remote_copy(
            src_ref=vals.at[slot], dst_ref=vals.at[slot], send_sem=v_send.at[to],
            recv_sem=v_recv.at[slot], device_id={"head": to}, device_id_type=MESH,
        )

    for o in range(1, n_head):
        value_copy(head, lax.rem(head + o, n_head)).start()
    for o in range(1, n_head):
        value_copy(lax.rem(head + o, n_head), lax.rem(head + o, n_head)).wait_recv()
    value_row = vals[0, 0:1, :]
    for o in range(1, n_head):
        value_row = value_row + vals[o, 0:1, :]
    value_out[...] = value_row
    res_row = value_row - target_ref[...]
    res = jnp.sum(jnp.where(eye, res_row, 0.0), axis=1, keepdims=True)

    for h in range(heads):
        a = att[h]
        w = weight_ref[:, cut(h)]
        inv = lax.rsqrt(jnp.mean(a * a, axis=1, keepdims=True) + EPSILON)
        aw = jnp.mean(a * w, axis=1, keepdims=True)
        ri = res * inv
        red[me, heads + h : heads + h + 1, :] = jnp.sum(a * ri, axis=0, keepdims=True)
        g = ri * (w - a * (inv * inv * aw))
        ga = (g * alive).astype(bf16)
        g_dir[h] = dot(ga, qd[h], 0, 0)
        if n_ctx > 1:
            @pl.when(ctx == n_ctx - 1)
            def _():
                for c in range(h * CUTS, (h + 1) * CUTS):
                    grad_copy(c).start()
        att[h] = g
    if n_ctx == 1:
        g_in[...] = jnp.zeros_like(g_in)
    else:
        @pl.when(ctx == n_ctx - 1)
        def _():
            g_in[...] = jnp.zeros_like(g_in)

    for h in range(heads):
        g = att[h]
        gb = g.astype(bf16)
        ga = (g * alive).astype(bf16)
        dp = jnp.where(live, dot(gb, v_ref[0, :, cut(h)], 1, 1), 0.0).astype(bf16)
        dq_dec = dot(dp, kd[h], 1, 0) + dot(ga, s_in[h].astype(bf16), 1, 0)
        dq_out[0, :, cut(h)] = (dq_dec * e_up[h]).astype(bf16)
        dqd[h] = dq_dec * qd[h].astype(f32)
        dkd[h] = dot(dp, qd[h], 0, 0)
        ptg[h] = dot(probs[h], gb, 0, 0)

    upper_b = jnp.where(rows <= cols, 1.0, 0.0).astype(bf16)
    for h in range(heads):
        if n_ctx > 1:
            for c in range(h * CUTS, (h + 1) * CUTS):
                part = (h, slice(c % CUTS * ROWS, (c % CUTS + 1) * ROWS))

                @pl.when(ctx < n_ctx - 1)
                def _():
                    grad_copy(c).wait_recv()

                @pl.when((ctx > 0) & (ctx < n_ctx - 1))
                def _():
                    g_dir[part] = g_in[part] * (last[h : h + 1, :] * alive_last) + g_dir[part]
                    grad_copy(c).start()

        up_last = last[h : h + 1, :]
        gs = g_in[h]
        gsb = gs.astype(bf16)
        dv_out[0, :, cut(h)] = (ptg[h] + dot(kt[h], gsb, 1, 1)).astype(bf16)
        tk = dot(vt[h], gsb, 1, 0) * up_last
        k_dec = kd[h].astype(f32)
        dk_dec = dkd[h] + tk
        dk_out[0, :, cut(h)] = (dk_dec * e_down[h]).astype(bf16)
        d_last = jnp.sum(k_dec * tk, axis=0, keepdims=True) + (
            jnp.sum(s_in[h] * gs, axis=0, keepdims=True) * (up_last * alive_last)
        )
        d_cum = dqd[h] - k_dec * dk_dec
        dx = (split_dot(upper_b, d_cum) + d_last) * slope[h]
        dg_out[0, :, cut(h)] = dx.astype(bf16)
        red[me, h : h + 1, :] = jnp.sum(dx, axis=0, keepdims=True)

    def red_copy(slot, to):
        return pltpu.make_async_remote_copy(
            src_ref=red.at[slot], dst_ref=red.at[slot], send_sem=r_send.at[to],
            recv_sem=r_recv.at[slot],
            device_id={"ctx": to // n_rep, "rep": lax.rem(to, n_rep)}, device_id_type=MESH,
        )

    for o in range(1, n_red):
        red_copy(me, lax.rem(me + o, n_red)).start()
    for o in range(1, n_red):
        other = lax.rem(me + o, n_red)
        red_copy(other, other).wait_recv()
    total = red[0]
    for o in range(1, n_red):
        total = total + red[o]
    total = total * (1.0 / (T * n_red))
    for h in range(heads):
        dbias_out[:, cut(h)] = total[h : h + 1, :]
        dweight_out[:, cut(h)] = total[heads + h : heads + h + 1, :]

    for o in range(1, n_red):
        red_copy(me, lax.rem(me + o, n_red)).wait_send()
    for o in range(1, n_head):
        value_copy(head, lax.rem(head + o, n_head)).wait_send()
    if n_ctx > 1:
        for h in range(CUTS * heads):
            @pl.when(ctx < n_ctx - 1)
            def _():
                state_copy(h).wait_send()

            @pl.when(ctx > 0)
            def _():
                grad_copy(h).wait_send()


def on_device(n_ctx, n_head, n_rep, *args):
    q, k, v, g, bias, weight, targets, kinds, starts = args
    T, width = q.shape[1], q.shape[2]
    heads = width // DK
    n_red = n_ctx * n_rep
    vm = pl.BlockSpec(memory_space=pltpu.VMEM)
    hbm = pl.BlockSpec(memory_space=pltpu.HBM)
    half = lambda: pltpu.VMEM((heads, T, DK), bf16)
    full = lambda: pltpu.VMEM((heads, T, DK), f32)
    sems = lambda n: pltpu.SemaphoreType.DMA((n,))
    row16 = jax.ShapeDtypeStruct((1, T, width), bf16)
    row = jax.ShapeDtypeStruct((1, width), f32)
    ins = (q, k, v, g, bias.reshape(1, width), weight.reshape(1, width), targets, kinds, starts)
    shapes = (jax.ShapeDtypeStruct((1, T), f32), row16, row16, row16, row16, row, row)
    outs = pl.pallas_call(
        functools.partial(kernel, n_ctx, n_head, n_rep, heads),
        out_shape=shapes,
        in_specs=[hbm] * 9,
        out_specs=(vm,) * 7,
        scratch_shapes=[
            *(pltpu.VMEM(a.shape, a.dtype) for a in ins), sems(9),
            half(), half(), half(), half(), pltpu.VMEM((heads, T, T), bf16),
            full(), full(), full(), full(), full(), full(), full(), full(),
            full(), full(), full(), pltpu.VMEM((8, DK), f32),
            pltpu.VMEM((n_head, 8, T), f32), pltpu.VMEM((n_red, 2 * heads, DK), f32),
            *(sems(CUTS * heads) for _ in range(4)),
            sems(n_head), sems(n_head), sems(n_red), sems(n_red),
        ],
        compiler_params=pltpu.CompilerParams(
            collective_id=0, has_side_effects=True, vmem_limit_bytes=54656 * 2**10
        ),
    )(*ins)
    value, dq, dk, dv, dg, dbias, dweight = outs
    return value, dq, dk, dv, dg, dbias.reshape(width), dweight.reshape(width)


def solution(mesh):
    rows = ("groups", "rep")
    full, tokens = P(rows, "ctx", "head"), P(rows, "ctx")
    sums = P(("groups", "head"))
    shape = mesh.shape
    return jax.shard_map(
        functools.partial(on_device, shape["ctx"], shape["head"], shape["rep"]),
        mesh=mesh,
        in_specs=(full, full, full, full, P("head"), P("head"), tokens, tokens, tokens),
        out_specs=(tokens, full, full, full, full, sums, sums),
        check_vma=False,
    )
```
